32 devices in a mesh: box: 8 (over z, x), dir: 4 (over y, core).
Axes of the slice: x: 2, y: 2, z: 4, core: 2. Of those that a mesh axis runs over, the one named last changes fastest.
Arguments:
- fine_out: bfloat16 [512, 32, 512], P(('box', 'dir')), may hold values from -6 to 6
- fine_list: int32 [512, 12], P(('box', 'dir')), may hold values from -1 to 511, as said below
- fine_slot: int32 [512], P('box'), may hold values from 0 to 3, as said below
- fine_translator: float32 [12, 2, 512], replicated, may hold values from -4 to 4
- theta_up_fine: bfloat16 [32, 16], replicated, may hold values from -1.5 to 1.5
- phi_up_fine: bfloat16 [64, 32], replicated, may hold values from -1 to 1
- middle_phase: float32 [4, 2048], replicated, may hold values from -3.140625 to 3.140625
- middle_list: int32 [128, 12], P('box'), may hold values from -1 to 127, as said below
- middle_slot: int32 [128], P('box'), may hold values from 0 to 3, as said below
- middle_translator: float32 [12, 2, 2048], P(None, None, 'dir'), may hold values from -2 to 2
- theta_up_middle: bfloat16 [64, 32], replicated, may hold values from -1 to 1
- phi_up_middle: bfloat16 [128, 64], replicated, may hold values from -0.75 to 0.75
- coarse_phase: float32 [4, 8192], replicated, may hold values from -3.140625 to 3.140625
- coarse_list: int32 [32, 12], replicated, may hold values from -1 to 31, as said below
- coarse_translator: float32 [12, 2, 8192], P(None, None, ('box', 'dir')), may hold values from -1.25 to 1.25
Outputs:
- fine_in: bfloat16 [512, 32, 512], P(('box', 'dir'))
- middle_in: bfloat16 [128, 32, 2048], P('box', None, 'dir')
- coarse_in: bfloat16 [32, 32, 8192], P(None, None, ('box', 'dir'))
The draws below stay inside these ranges and needn't reach their ends.
Inputs may be any that keep to these rules, and one draw needn't show every extreme that they name: `fine_list`: row i names distinct fine boxes j with 2 <= |j - i| <= 7 and |j // 4 - i // 4| <= 1, in any slots; -1 marks an empty slot. `middle_list`: row i names distinct middle boxes j with 2 <= |j - i| <= 7 and |j // 4 - i // 4| <= 1, in any slots; -1 marks an empty slot. `coarse_list`: row i names distinct coarse boxes j with 2 <= |j - i| <= 7 and |j // 4 - i // 4| <= 1, in any slots; -1 marks an empty slot. `fine_slot`: the parent of fine box c is middle box c // 4; each aligned group of 4 fine boxes takes each of the values 0 to 3 once. `middle_slot`: the parent of middle box m is coarse box m // 4; each aligned group of 4 middle boxes takes each of the values 0 to 3 once.
All inputs are finite; a program needn't handle non-finite values.
Results may differ from the reference program's by a relative error of at most 0.007.
Values may be sent and summed in bfloat16 or wider, within the bound.
A program may use at most 64 MiB of HBM per device.

```python
import jax
import jax.numpy as jnp
from jax import lax

MAX_OFFSET = 7
THETA_FINE = 16
PHI_FINE = 32
THETA_MID = 32
PHI_MID = 64
THETA_COARSE = 64
PHI_COARSE = 128
COMPONENTS = 32
LIST_SLOTS = 12
DIRS_FINE = 512
DIRS_MID = 2048
DIRS_COARSE = 8192
FINE_BOXES = 512
MID_BOXES = 128
COARSE_BOXES = 32


def offset_table():
    return jnp.array(list(range(-MAX_OFFSET, -1)) + list(range(2, MAX_OFFSET + 1)), dtype=jnp.int32)


def draw_list_rows(base_key, box_count):
    region_key = jax.random.fold_in(base_key, 11)
    occupy_key = jax.random.fold_in(base_key, 12)
    shuffle_key = jax.random.fold_in(base_key, 13)
    centre = jnp.arange(box_count, dtype=jnp.int32)[:, None]
    target = centre + offset_table()[None, :]
    inside = (target >= 0) & (target < box_count) & (jnp.abs(target // 4 - centre // 4) <= 1)
    region_count = (box_count + 15) // 16
    density = jax.random.randint(region_key, (region_count,), 1, 5, dtype=jnp.int32)
    levels = jax.random.randint(occupy_key, (box_count,), 0, 4, dtype=jnp.int32)
    occupied = levels < jnp.repeat(density, 16)[:box_count]
    clipped = jnp.clip(target, 0, box_count - 1)
    present = inside & occupied[clipped] & occupied[centre]
    listed = jnp.where(present, target, -1)
    scores = jax.random.randint(shuffle_key, listed.shape, 0, 1 << 20, dtype=jnp.int32) * LIST_SLOTS + jnp.arange(LIST_SLOTS, dtype=jnp.int32)[None, :]
    slot_order = jnp.argsort(scores, axis=1, stable=True)
    return jnp.take_along_axis(listed, slot_order, axis=1).astype(jnp.int32)


def draw_child_slots(base_key, box_count):
    scores = jax.random.randint(base_key, (box_count // 4, 4), 0, 1 << 20, dtype=jnp.int32) * 4 + jnp.arange(4, dtype=jnp.int32)[None, :]
    return jnp.argsort(scores, axis=1, stable=True).reshape(box_count).astype(jnp.int32)


def draw_fine_list(key, part):
    return draw_list_rows(jax.random.fold_in(key, 1), FINE_BOXES)


def draw_middle_list(key, part):
    return draw_list_rows(jax.random.fold_in(key, 2), MID_BOXES)


def draw_coarse_list(key, part):
    return draw_list_rows(jax.random.fold_in(key, 3), COARSE_BOXES)


def draw_fine_slot(key, part):
    return draw_child_slots(jax.random.fold_in(key, 4), FINE_BOXES)


def draw_middle_slot(key, part):
    return draw_child_slots(jax.random.fold_in(key, 5), MID_BOXES)


def shard_levels(rng, extent, pieces, smallest, top_value):
    factor_of = 1.0
    for dim, blocks in pieces:
        heights = jax.random.uniform(jax.random.fold_in(jax.random.fold_in(rng, 6), dim), (blocks,), jnp.float32, smallest / len(pieces), top_value / len(pieces))
        factor_of = factor_of * jnp.repeat(jnp.exp(heights), extent[dim] // blocks).reshape((-1,) + (1,) * (len(extent) - 1 - dim))
    return factor_of


def scatter_about(stream_key, shape, scale, most, shards=(), kind=jnp.bfloat16):
    drawn = scale * jax.random.normal(stream_key, shape, jnp.float32)
    if shards:
        drawn = drawn * shard_levels(stream_key, shape, shards, -0.22, 0.18)
    return jnp.clip(drawn, -most, most).astype(kind)


def setup_inputs(seed: int = 0) -> dict:
    key_list = jax.random.split(jax.random.key(seed), 16)
    return {
        "fine_out": scatter_about(key_list[0], (FINE_BOXES, COMPONENTS, DIRS_FINE), 1.0, 6.0, ((0, 32),)),
        "fine_list": draw_fine_list(jax.random.fold_in(key_list[15], 71), 0),
        "fine_slot": draw_fine_slot(jax.random.fold_in(key_list[15], 71), 0),
        "fine_translator": scatter_about(key_list[3], (LIST_SLOTS, 2, DIRS_FINE), 0.3, 4.0, (), jnp.float32),
        "theta_up_fine": scatter_about(key_list[4], (THETA_MID, THETA_FINE), THETA_FINE ** -0.5, 1.5),
        "phi_up_fine": scatter_about(key_list[5], (PHI_MID, PHI_FINE), PHI_FINE ** -0.5, 1.0),
        "middle_phase": jnp.clip(jax.random.uniform(key_list[6], (4, DIRS_MID), jnp.float32, -3.140625, 3.140625), -3.140625, 3.140625),
        "middle_list": draw_middle_list(jax.random.fold_in(key_list[15], 71), 0),
        "middle_slot": draw_middle_slot(jax.random.fold_in(key_list[15], 71), 0),
        "middle_translator": scatter_about(key_list[9], (LIST_SLOTS, 2, DIRS_MID), 0.15, 2.0, ((2, 4),), jnp.float32),
        "theta_up_middle": scatter_about(key_list[10], (THETA_COARSE, THETA_MID), THETA_MID ** -0.5, 1.0),
        "phi_up_middle": scatter_about(key_list[11], (PHI_COARSE, PHI_MID), PHI_MID ** -0.5, 0.75),
        "coarse_phase": jnp.clip(jax.random.uniform(key_list[12], (4, DIRS_COARSE), jnp.float32, -3.140625, 3.140625), -3.140625, 3.140625),
        "coarse_list": draw_coarse_list(jax.random.fold_in(key_list[15], 71), 0),
        "coarse_translator": scatter_about(key_list[14], (LIST_SLOTS, 2, DIRS_COARSE), 0.08, 1.25, ((2, 32),), jnp.float32),
    }


def complex_times(real_part, imag_part, pattern):
    half_size = pattern.shape[-2] // 2
    pattern_real = pattern[..., :half_size, :]
    pattern_imag = pattern[..., half_size:, :]
    return jnp.concatenate([real_part * pattern_real - imag_part * pattern_imag, real_part * pattern_imag + imag_part * pattern_real], axis=-2)


def offsets_used():
    return list(range(-MAX_OFFSET, -1)) + list(range(2, MAX_OFFSET + 1))


def translate_rows(padded, entries, first_box, translator):
    row_count = entries.shape[0]
    box_ids = first_box + jnp.arange(row_count, dtype=jnp.int32)
    summed = jnp.zeros((row_count,) + padded.shape[1:], jnp.float32)
    for slot_index, offset in enumerate(offsets_used()):
        present = jnp.any(entries == (box_ids + offset)[:, None], axis=1).astype(jnp.float32)
        source = padded[MAX_OFFSET + offset:MAX_OFFSET + offset + row_count].astype(jnp.float32)
        contrib = complex_times(translator[slot_index, 0], translator[slot_index, 1], source)
        summed = summed + present[:, None, None] * contrib
    return summed


def interpolate(pattern, theta_matrix, phi_matrix):
    box_count, part_count = pattern.shape[0], pattern.shape[1]
    sample_grid = pattern.reshape(box_count * part_count, theta_matrix.shape[1], phi_matrix.shape[1]).astype(jnp.float32)
    along_phi = jnp.einsum("nap,qp->naq", sample_grid, phi_matrix.astype(jnp.float32), precision=lax.Precision.HIGHEST)
    along_phi = lax.optimization_barrier(along_phi.astype(jnp.bfloat16)).astype(jnp.float32)
    lifted = jnp.einsum("naq,ta->ntq", along_phi, theta_matrix.astype(jnp.float32), precision=lax.Precision.HIGHEST)
    return lifted.reshape(box_count, part_count, -1)


def phase_shift(values, slot_ids, angles):
    choose = (slot_ids[:, None] == jnp.arange(4, dtype=jnp.int32)[None, :]).astype(jnp.float32)
    cosine = jnp.dot(choose, jnp.cos(angles), precision=lax.Precision.HIGHEST)
    sine_part = jnp.dot(choose, jnp.sin(angles), precision=lax.Precision.HIGHEST)
    return complex_times(cosine[:, None, :], sine_part[:, None, :], values)


def sum_children(values):
    return values.reshape(values.shape[0] // 4, 4, values.shape[1], values.shape[2]).sum(axis=1)


def reference(fine_out, fine_list, fine_slot, fine_translator, theta_up_fine, phi_up_fine, middle_phase, middle_list, middle_slot, middle_translator, theta_up_middle, phi_up_middle, coarse_phase, coarse_list, coarse_translator):
    fine_pad = jnp.pad(fine_out, ((MAX_OFFSET, MAX_OFFSET), (0, 0), (0, 0)))
    fine_in = translate_rows(fine_pad, fine_list, 0, fine_translator).astype(jnp.bfloat16)

    def climb_tree(inputs):
        children, child_slots, parent_slots = inputs
        lifted = interpolate(children, theta_up_fine, phi_up_fine)
        parents = sum_children(phase_shift(lifted, child_slots, middle_phase)).astype(jnp.bfloat16)
        raised = interpolate(parents, theta_up_middle, phi_up_middle)
        coarse = sum_children(phase_shift(raised, parent_slots, coarse_phase)).astype(jnp.bfloat16)
        return parents, coarse

    middle_blocks, coarse_blocks = lax.map(climb_tree, (fine_out.reshape(COARSE_BOXES, 16, COMPONENTS, DIRS_FINE), fine_slot.reshape(COARSE_BOXES, 16), middle_slot.reshape(COARSE_BOXES, 4)))
    middle_out = middle_blocks.reshape(MID_BOXES, COMPONENTS, DIRS_MID)
    coarse_out = coarse_blocks.reshape(COARSE_BOXES, COMPONENTS, DIRS_COARSE)
    middle_pad = jnp.pad(middle_out, ((MAX_OFFSET, MAX_OFFSET), (0, 0), (0, 0)))
    middle_in = translate_rows(middle_pad, middle_list, 0, middle_translator).astype(jnp.bfloat16)
    coarse_pad = jnp.pad(coarse_out, ((MAX_OFFSET, MAX_OFFSET), (0, 0), (0, 0)))
    coarse_in = translate_rows(coarse_pad, coarse_list, 0, coarse_translator).astype(jnp.bfloat16)
    return (fine_in, middle_in, coarse_in)
```

```python
import functools

import jax
import jax.numpy as jnp
from jax import lax
from jax.experimental import pallas as pl
from jax.experimental.pallas import tpu as pltpu
from jax.sharding import PartitionSpec as P

MAX_OFFSET = 7
LANES = 128
F32 = jnp.float32
BF16 = jnp.bfloat16
MESH = pl.DeviceIdType.MESH


def offsets_used():
    return list(range(-MAX_OFFSET, -1)) + list(range(2, MAX_OFFSET + 1))


def presence(entries, first_box):
    ids = first_box + jnp.arange(entries.shape[0], dtype=jnp.int32)
    wanted = ids[:, None] + jnp.array(offsets_used(), jnp.int32)[None, :]
    return jnp.any(entries[:, None, :] == wanted[:, :, None], axis=2).astype(F32)


def iota(shape, dim):
    return lax.broadcasted_iota(jnp.int32, shape, dim)


def one_hot(cond):
    return jnp.where(cond, 1.0, 0.0).astype(BF16)


def dot(a, b, dims=((1,), (0,))):
    return lax.dot_general(a, b, (dims, ((), ())), preferred_element_type=F32)


def kron_identity(matrix, width):
    rows, cols = matrix.shape
    shift = width.bit_length() - 1
    left = one_hot((iota((rows * width, rows), 0) >> shift) == iota((rows * width, rows), 1))
    right = one_hot(iota((cols, cols * width), 0) == (iota((cols, cols * width), 1) >> shift))
    full = dot(dot(left, matrix).astype(BF16), right)
    shape = (rows * width, cols * width)
    keep = (iota(shape, 0) & (width - 1)) == (iota(shape, 1) & (width - 1))
    return jnp.where(keep, full, 0.0).astype(BF16)


def phi_blocks(phi, pair):
    q, p = phi.shape
    thetas = 256 // (pair * p)
    rows, cols = pair * thetas * p, thetas * pair * q
    left = one_hot((iota((rows, p), 0) & (p - 1)) == iota((rows, p), 1))
    right = one_hot(iota((q, cols), 0) == (iota((q, cols), 1) & (q - 1)))
    full = dot(dot(left, phi, ((1,), (1,))).astype(BF16), right)
    shape = (rows, cols)
    r, c = iota(shape, 0), iota(shape, 1)
    ps, qs = p.bit_length() - 1, q.bit_length() - 1
    ths, prs = thetas.bit_length() - 1, pair.bit_length() - 1
    row_t, row_h = (r >> ps) & (thetas - 1), r >> (ps + ths)
    col_h, col_t = (c >> qs) & (pair - 1), c >> (qs + prs)
    return jnp.where((row_t == col_t) & (row_h == col_h), full, 0.0).astype(BF16)


def translate(groups, tiles, load, mask_ref, factor, store):
    def step(it, _):
        g, lt = lax.div(it, tiles), lax.rem(it, tiles)
        sources = [load(g, j, lt).astype(F32) for j in range(12)]
        half = sources[0].shape[0] // 2
        for i in range(4):
            real, imag = None, None
            for s, offset in enumerate(offsets_used()):
                j = 4 + i + offset
                if j < 0 or j > 11:
                    continue
                m = mask_ref[4 * g + i, s]
                a, b = factor(s, 0, lt) * m, factor(s, 1, lt) * m
                pr, pi = sources[j][:half], sources[j][half:]
                tr, ti = a * pr - b * pi, a * pi + b * pr
                real = tr if real is None else real + tr
                imag = ti if imag is None else imag + ti
            store(4 * g + i, lt, real.astype(BF16), imag.astype(BF16))
        return 0

    lax.fori_loop(0, groups * tiles, step, 0)


def lane_tile(lt):
    return pl.ds(pl.multiple_of(lt * LANES, LANES), LANES)


def kernel(
    nb, nd,
    fine_hbm, fine_mask, fine_slot, fine_tr, theta_f, phi_f, mid_phase,
    mid_mask, mid_slot, mid_tr, theta_m, phi_m, coarse_phase, coarse_mask, coarse_tr,
    fine_in, mid_in, coarse_in,
    fpad, par, mrecv, crs, crecv, along1, lift1, along2, lift2,
    cosm, sinm, cosc, sinc,
    load_sem, fsend, frecv, msend, mrecv_sem, csend, crecv_sem,
):
    n = nb * nd
    b, d = lax.axis_index("box"), lax.axis_index("dir")
    me = b * nd + d
    held = fine_in.shape[0]
    t_mid, t_coarse = theta_f.shape[0], theta_m.shape[0]
    mid_tiles = par.shape[0]
    mlt = mid_tiles // nd
    ctiles = crecv.shape[1]
    ntile = t_coarse // ctiles
    share = n // ntile

    def device(i):
        return (lax.div(i, nd), lax.rem(i, nd))

    fine_load = pltpu.make_async_copy(fine_hbm, fpad.at[pl.ds(4, held)], load_sem)
    fine_load.start()
    barrier = pltpu.get_barrier_semaphore()

    def greet(j, _):
        pl.semaphore_signal(
            barrier, inc=1, device_id=device(lax.rem(me + 1 + j, n)), device_id_type=MESH
        )
        return 0

    lax.fori_loop(0, n - 1, greet, 0)

    bd1 = phi_blocks(phi_f[...], 2)
    k1 = kron_identity(theta_f[...], 16)
    bd2 = phi_blocks(phi_m[...], 1)
    k2 = kron_identity(theta_m[...], 8)
    cosc[...] = jnp.cos(coarse_phase[...])
    sinc[...] = jnp.sin(coarse_phase[...])
    cosine, sine = jnp.cos(mid_phase[...]), jnp.sin(mid_phase[...])
    low = iota((t_mid, LANES), 1) < LANES // 2
    for u in range(2):
        for k in range(4):
            s0 = fine_slot[d * held + 8 * u + k]
            s1 = fine_slot[d * held + 8 * u + 4 + k]
            for table, values in ((cosm, cosine), (sinm, sine)):
                first = values[3]
                second = values[3]
                for s in range(3):
                    first = jnp.where(s0 == s, values[s], first)
                    second = jnp.where(s1 == s, values[s], second)
                table[4 * u + k] = jnp.where(low, first, second)

    zeros4 = jnp.zeros((4,) + fpad.shape[1:], BF16)

    @pl.when(me == 0)
    def _():
        fpad[0:4] = zeros4

    @pl.when(me == n - 1)
    def _():
        fpad[4 + held:8 + held] = zeros4

    @pl.when(b == 0)
    def _():
        mrecv[0] = jnp.zeros(mrecv.shape[1:], BF16)

    @pl.when(b == nb - 1)
    def _():
        mrecv[nd + 1] = jnp.zeros(mrecv.shape[1:], BF16)

    crecv[0:4] = jnp.zeros((4,) + crecv.shape[1:], BF16)
    crecv[n + 4:n + 8] = jnp.zeros((4,) + crecv.shape[1:], BF16)

    fine_load.wait()

    for g in range(4):
        part = fpad[4:4 + held, :, g * LANES:(g + 1) * LANES]
        part = part.reshape(held // 8, 2, 4 * 32, LANES)
        pair = jnp.concatenate([part[:, 0], part[:, 1]], axis=-1).reshape(-1, 2 * LANES)
        out = dot(pair, bd1).astype(BF16)
        for i in range(4):
            along1[4 * g + i] = out[:, i * LANES:(i + 1) * LANES]
    for uk in range(8):
        rhs = jnp.concatenate(
            [
                along1[:, uk * 32:uk * 32 + 16, :].reshape(256, LANES),
                along1[:, uk * 32 + 16:uk * 32 + 32, :].reshape(256, LANES),
            ],
            axis=-1,
        )
        lift1[uk] = dot(k1, rhs).reshape(t_mid, 16, 2 * LANES)

    lower = iota((16, LANES), 1) < LANES // 2

    def parents_step(v, _):
        for u in range(2):
            sums = []
            for e in range(2):
                t2 = 2 * v + e
                real, imag = None, None
                for k in range(4):
                    uk = 4 * u + k
                    value = lift1[uk, t2]
                    vr, vi = value[:, :LANES], value[:, LANES:]
                    co = cosm[uk, pl.ds(t2, 1), :]
                    si = sinm[uk, pl.ds(t2, 1), :]
                    tr, ti = co * vr - si * vi, co * vi + si * vr
                    real = tr if real is None else real + tr
                    imag = ti if imag is None else imag + ti
                sums.append((real, imag))
            for c in range(2):
                s0, s1 = sums[0][c], sums[1][c]
                par[v, 2 * u, 16 * c:16 * c + 16, :] = jnp.where(
                    lower, s0, pltpu.roll(s1, LANES // 2, 1)
                ).astype(BF16)
                par[v, 2 * u + 1, 16 * c:16 * c + 16, :] = jnp.where(
                    lower, pltpu.roll(s0, LANES // 2, 1), s1
                ).astype(BF16)
        return 0

    lax.fori_loop(0, mid_tiles, parents_step, 0)

    pl.semaphore_wait(barrier, n - 1)

    def fine_copy(to_next):
        peer = me + 1 if to_next else me - 1
        return pltpu.make_async_remote_copy(
            src_ref=fpad.at[pl.ds(held, 4)] if to_next else fpad.at[pl.ds(4, 4)],
            dst_ref=fpad.at[pl.ds(0, 4)] if to_next else fpad.at[pl.ds(4 + held, 4)],
            send_sem=fsend.at[0 if to_next else 1],
            recv_sem=frecv.at[0 if to_next else 1],
            device_id=device(peer),
            device_id_type=MESH,
        )

    def mid_copy(dd, box, slot, sem):
        return pltpu.make_async_remote_copy(
            src_ref=par.at[pl.ds(dd * mlt, mlt)],
            dst_ref=mrecv.at[slot],
            send_sem=msend.at[sem],
            recv_sem=mrecv_sem.at[slot],
            device_id=(box, dd),
            device_id_type=MESH,
        )

    def coarse_copy(tile, dest):
        return pltpu.make_async_remote_copy(
            src_ref=crs.at[pl.ds(tile * ctiles, ctiles)],
            dst_ref=crecv.at[4 + me],
            send_sem=csend.at[dest],
            recv_sem=crecv_sem.at[me],
            device_id=device(dest),
            device_id_type=MESH,
        )

    def each_mid(act):
        def own(j, _):
            dd = lax.rem(d + 1 + j, nd)
            act(mid_copy(dd, b, 1 + d, dd))
            return 0

        lax.fori_loop(0, nd - 1, own, 0)

        @pl.when((d == nd - 1) & (b < nb - 1))
        def _():
            def up(dd, _):
                act(mid_copy(dd, b + 1, 0, nd + dd))
                return 0

            lax.fori_loop(0, nd, up, 0)

        @pl.when((d == 0) & (b > 0))
        def _():
            def down(dd, _):
                act(mid_copy(dd, b - 1, nd + 1, nd + dd))
                return 0

            lax.fori_loop(0, nd, down, 0)

    each_mid(lambda c: c.start())
    mrecv[1 + d] = par[pl.ds(d * mlt, mlt)]

    @pl.when(me < n - 1)
    def _():
        fine_copy(True).start()

    @pl.when(me > 0)
    def _():
        fine_copy(False).start()

    rows = par.shape[1] * par.shape[2]
    for g in range(mid_tiles // 2):
        lhs = jnp.concatenate(
            [par[2 * g].reshape(rows, LANES), par[2 * g + 1].reshape(rows, LANES)], axis=-1
        )
        out = dot(lhs, bd2)
        for i in range(4):
            along2[4 * g + i] = out[:, i * LANES:(i + 1) * LANES]
    for k in range(4):
        for cg in range(2):
            r0 = k * 32 + cg * 8
            rhs = jnp.concatenate(
                [
                    along2[:, r0:r0 + 8, :].reshape(256, LANES),
                    along2[:, r0 + 16:r0 + 24, :].reshape(256, LANES),
                ],
                axis=-1,
            ).astype(BF16)
            lift2[2 * k + cg] = dot(k2, rhs).reshape(t_coarse, 8, 2 * LANES)

    slots = [mid_slot[d * 4 + k] for k in range(4)]
    my_tile = lax.div(me, share)

    def coarse_step(j, _):
        tile = lax.rem(my_tile + 1 + j, ntile)
        for i in range(ctiles):
            t2 = tile * ctiles + i
            reals, imags = [None, None], [None, None]
            for k in range(4):
                co = cosc[slots[k], pl.ds(t2, 1), :]
                si = sinc[slots[k], pl.ds(t2, 1), :]
                for cg in range(2):
                    value = lift2[2 * k + cg, t2]
                    vr, vi = value[:, :LANES], value[:, LANES:]
                    tr, ti = co * vr - si * vi, co * vi + si * vr
                    reals[cg] = tr if k == 0 else reals[cg] + tr
                    imags[cg] = ti if k == 0 else imags[cg] + ti
            crs[t2, 0:16, :] = jnp.concatenate(reals, axis=0).astype(BF16)
            crs[t2, 16:32, :] = jnp.concatenate(imags, axis=0).astype(BF16)
        for r in range(share):
            dest = tile * share + r

            @pl.when(dest != me)
            def _():
                coarse_copy(tile, dest).start()

        return 0

    lax.fori_loop(0, ntile, coarse_step, 0)
    crecv[4 + me] = crs[pl.ds(my_tile * ctiles, ctiles)]

    @pl.when(me > 0)
    def _():
        fine_copy(True).wait_recv()

    @pl.when(me < n - 1)
    def _():
        fine_copy(False).wait_recv()

    def fine_store(i, lt, real, imag):
        fine_in[i, 0:16, lane_tile(lt)] = real
        fine_in[i, 16:32, lane_tile(lt)] = imag

    translate(
        held // 4,
        fine_in.shape[2] // LANES,
        lambda g, j, lt: fpad[4 * g + j, :, lane_tile(lt)],
        fine_mask,
        lambda s, c, lt: fine_tr[s, c:c + 1, lane_tile(lt)],
        fine_store,
    )

    def mid_wait(slot):
        mid_copy(0, b, slot, 0).wait_recv()

    def own_wait(j, _):
        mid_wait(1 + lax.rem(d + 1 + j, nd))
        return 0

    lax.fori_loop(0, nd - 1, own_wait, 0)

    @pl.when(b > 0)
    def _():
        mid_wait(0)

    @pl.when(b < nb - 1)
    def _():
        mid_wait(nd + 1)

    def mid_store(i, lt, real, imag):
        mid_in[i, 0:16, lane_tile(lt)] = real
        mid_in[i, 16:32, lane_tile(lt)] = imag

    translate(
        nd,
        mlt,
        lambda g, j, lt: mrecv[g + j // 4, lt, j % 4],
        mid_mask,
        lambda s, c, lt: mid_tr[s, c:c + 1, lane_tile(lt)],
        mid_store,
    )

    def coarse_wait(j, _):
        source = lax.rem(me + n - 1 - j, n)
        pltpu.make_async_remote_copy(
            src_ref=crs.at[pl.ds(0, ctiles)],
            dst_ref=crecv.at[4 + source],
            send_sem=csend.at[source],
            recv_sem=crecv_sem.at[source],
            device_id=device(source),
            device_id_type=MESH,
        ).wait_recv()
        return 0

    lax.fori_loop(0, n - 1, coarse_wait, 0)

    width = coarse_in.shape[2]
    if share == 1:

        def coarse_load(g, j, lt):
            return crecv[4 * g + j, lt]

        def coarse_store(i, lt, real, imag):
            coarse_in[i, 0:16, lane_tile(lt)] = real
            coarse_in[i, 16:32, lane_tile(lt)] = imag

        def coarse_factor(s, c, lt):
            return coarse_tr[s, c:c + 1, lane_tile(lt)]

    else:
        turn = lax.rem(LANES - lax.rem(me, share) * width, LANES)

        def coarse_load(g, j, lt):
            return pltpu.roll(crecv[4 * g + j, lt].astype(F32), turn, 1)[:, :width]

        def coarse_store(i, lt, real, imag):
            coarse_in[i, 0:16, :] = real
            coarse_in[i, 16:32, :] = imag

        def coarse_factor(s, c, lt):
            return coarse_tr[s, c:c + 1, :]

    translate(n // 4, ctiles, coarse_load, coarse_mask, coarse_factor, coarse_store)

    each_mid(lambda c: c.wait_send())

    @pl.when(me < n - 1)
    def _():
        fine_copy(True).wait_send()

    @pl.when(me > 0)
    def _():
        fine_copy(False).wait_send()

    def sent(j, _):
        dest = lax.rem(me + 1 + j, n)
        coarse_copy(lax.div(dest, share), dest).wait_send()
        return 0

    lax.fori_loop(0, n - 1, sent, 0)


def local(
    nb, nd,
    fine_out, fine_list, fine_slot, fine_translator, theta_up_fine, phi_up_fine, middle_phase,
    middle_list, middle_slot, middle_translator, theta_up_middle, phi_up_middle, coarse_phase,
    coarse_list, coarse_translator,
):
    n = nb * nd
    b, d = lax.axis_index("box"), lax.axis_index("dir")
    held, comps, fine_dirs = fine_out.shape
    fine_mask = presence(fine_list, (b * nd + d) * held)
    mid_mask = presence(middle_list, b * middle_list.shape[0])
    coarse_mask = presence(coarse_list, 0)
    t_mid, q_mid = theta_up_fine.shape[0], phi_up_fine.shape[0]
    t_coarse, q_coarse = theta_up_middle.shape[0], phi_up_middle.shape[0]
    mid_phase = middle_phase.reshape(4, t_mid, q_mid)
    mid_phase = jnp.concatenate([mid_phase, mid_phase], axis=-1)
    co_phase = coarse_phase.reshape(4, t_coarse, q_coarse)
    mid_tiles = t_mid * q_mid // LANES
    width = coarse_translator.shape[2]
    ctiles = max(1, width // LANES)
    vmem = pl.BlockSpec(memory_space=pltpu.VMEM)
    smem = pl.BlockSpec(memory_space=pltpu.SMEM)
    dma = pltpu.SemaphoreType.DMA
    return pl.pallas_call(
        functools.partial(kernel, nb, nd),
        out_shape=(
            jax.ShapeDtypeStruct(fine_out.shape, BF16),
            jax.ShapeDtypeStruct((middle_list.shape[0], comps, middle_translator.shape[2]), BF16),
            jax.ShapeDtypeStruct((coarse_list.shape[0], comps, width), BF16),
        ),
        in_specs=[
            pl.BlockSpec(memory_space=pl.ANY), smem, smem, vmem, vmem, vmem, vmem,
            smem, smem, vmem, vmem, vmem, vmem, smem, vmem,
        ],
        out_specs=(vmem, vmem, vmem),
        scratch_shapes=[
            pltpu.VMEM((held + 8, comps, fine_dirs), BF16),
            pltpu.VMEM((mid_tiles, 4, comps, LANES), BF16),
            pltpu.VMEM((nd + 2, mid_tiles // nd, 4, comps, LANES), BF16),
            pltpu.VMEM((t_coarse, comps, LANES), BF16),
            pltpu.VMEM((n + 8, ctiles, comps, LANES), BF16),
            pltpu.VMEM((theta_up_fine.shape[1], held // 2 * comps, LANES), BF16),
            pltpu.VMEM((held // 2, t_mid, 16, 2 * LANES), F32),
            pltpu.VMEM((theta_up_middle.shape[1], 4 * comps, LANES), F32),
            pltpu.VMEM((8, t_coarse, 8, 2 * LANES), F32),
            pltpu.VMEM((held // 2, t_mid, LANES), F32),
            pltpu.VMEM((held // 2, t_mid, LANES), F32),
            pltpu.VMEM((4, t_coarse, LANES), F32),
            pltpu.VMEM((4, t_coarse, LANES), F32),
            dma, dma((2,)), dma((2,)), dma((2 * nd,)), dma((nd + 2,)), dma((n,)), dma((n,)),
        ],
        compiler_params=pltpu.CompilerParams(
            collective_id=0, has_side_effects=True, vmem_limit_bytes=48 * 1024 * 1024
        ),
        cost_estimate=pl.CostEstimate(
            flops=4_000_000_000, bytes_accessed=4_000_000, transcendentals=0
        ),
    )(
        fine_out, fine_mask, fine_slot, fine_translator, theta_up_fine, phi_up_fine, mid_phase,
        mid_mask, middle_slot, middle_translator, theta_up_middle, phi_up_middle, co_phase,
        coarse_mask, coarse_translator,
    )


def solution(mesh):
    return jax.shard_map(
        functools.partial(local, mesh.shape["box"], mesh.shape["dir"]),
        mesh=mesh,
        in_specs=(
            P(("box", "dir"), None, None),
            P(("box", "dir"), None),
            P("box"),
            P(),
            P(),
            P(),
            P(),
            P("box", None),
            P("box"),
            P(None, None, "dir"),
            P(),
            P(),
            P(),
            P(),
            P(None, None, ("box", "dir")),
        ),
        out_specs=(
            P(("box", "dir"), None, None),
            P("box", None, "dir"),
            P(None, None, ("box", "dir")),
        ),
        check_vma=False,
    )
```

```python
import functools

import jax
import jax.numpy as jnp
from jax import lax
from jax.experimental import pallas as pl
from jax.experimental.pallas import tpu as pltpu
from jax.sharding import PartitionSpec as P

MAX_OFFSET = 7
LANES = 128
F32 = jnp.float32
BF16 = jnp.bfloat16
MESH = pl.DeviceIdType.MESH


def offsets_used():
    return list(range(-MAX_OFFSET, -1)) + list(range(2, MAX_OFFSET + 1))


def iota(shape, dim):
    return lax.broadcasted_iota(jnp.int32, shape, dim)


def one_hot(cond):
    return jnp.where(cond, 1.0, 0.0).astype(BF16)


def dot(a, b, dims=((1,), (0,))):
    return lax.dot_general(a, b, (dims, ((), ())), preferred_element_type=F32)


def kron_identity(matrix, width):
    cols, rows = matrix.shape
    shift = width.bit_length() - 1
    left = one_hot((iota((rows * width, rows), 0) >> shift) == iota((rows * width, rows), 1))
    right = one_hot(iota((cols, cols * width), 0) == (iota((cols, cols * width), 1) >> shift))
    full = dot(dot(left, matrix, ((1,), (1,))).astype(BF16), right)
    shape = (rows * width, cols * width)
    keep = (iota(shape, 0) & (width - 1)) == (iota(shape, 1) & (width - 1))
    return jnp.where(keep, full, 0.0).astype(BF16)


def phi_blocks(phi, pair):
    p, q = phi.shape
    thetas = 256 // (pair * p)
    rows, cols = pair * thetas * p, thetas * pair * q
    left = one_hot((iota((rows, p), 0) & (p - 1)) == iota((rows, p), 1))
    right = one_hot(iota((q, cols), 0) == (iota((q, cols), 1) & (q - 1)))
    full = dot(dot(left, phi).astype(BF16), right)
    shape = (rows, cols)
    r, c = iota(shape, 0), iota(shape, 1)
    ps, qs = p.bit_length() - 1, q.bit_length() - 1
    ths, prs = thetas.bit_length() - 1, pair.bit_length() - 1
    row_t, row_h = (r >> ps) & (thetas - 1), r >> (ps + ths)
    col_h, col_t = (c >> qs) & (pair - 1), c >> (qs + prs)
    return jnp.where((row_t == col_t) & (row_h == col_h), full, 0.0).astype(BF16)


def spread(mask, s, column):
    rows = column.shape[0]
    mask[s] = jnp.broadcast_to(column[:, :, None], (rows, 8, LANES))


def row_presence(mask, entries, first_box):
    ids = first_box + iota(entries.shape, 0)
    for s, offset in enumerate(offsets_used()):
        hit = jnp.where(entries == ids + offset, 1.0, 0.0)
        spread(mask, s, jnp.max(hit, axis=1, keepdims=True))


def column_presence(mask, entries):
    count = entries.shape[1]
    ids = iota(entries.shape, 1)
    eye = iota((count, count), 0) == iota((count, count), 1)
    for s, offset in enumerate(offsets_used()):
        hit = jnp.where(entries == ids + offset, 1.0, 0.0)
        row = jnp.max(hit, axis=0, keepdims=True)
        spread(mask, s, jnp.sum(jnp.where(eye, row, 0.0), axis=1, keepdims=True))


def repeat_rows(wide, factors):
    for s in range(factors.shape[0]):
        for c in range(2):
            wide[s, c] = jnp.broadcast_to(factors[s, c:c + 1, :], wide.shape[2:])


def pack_rows(table):
    half = table.shape[0] // 2
    return jnp.concatenate([table[:half], table[half:]], axis=1)


def translate(groups, tiles, load, mask_ref, factor, store):
    def step(it, _):
        g, lt = lax.div(it, tiles), lax.rem(it, tiles)
        sources = [load(g, j, lt).astype(F32) for j in range(12)]
        sources = [x.reshape(4, 8, x.shape[1]) for x in sources]
        width = sources[0].shape[2]
        for i in range(4):
            real, imag = None, None
            for s, offset in enumerate(offsets_used()):
                j = 4 + i + offset
                if j < 0 or j > 11:
                    continue
                m = mask_ref[s, 4 * g + i][:, :width]
                a, b = factor(s, 0, lt) * m, factor(s, 1, lt) * m
                pr, pi = sources[j][:2], sources[j][2:]
                tr, ti = a * pr - b * pi, a * pi + b * pr
                real = tr if real is None else real + tr
                imag = ti if imag is None else imag + ti
            real, imag = real.reshape(16, width), imag.reshape(16, width)
            store(4 * g + i, lt, real.astype(BF16), imag.astype(BF16))
        return 0

    lax.fori_loop(0, groups * tiles, step, 0)


def lane_tile(lt):
    return pl.ds(pl.multiple_of(lt * LANES, LANES), LANES)


def kernel(
    nb, nd,
    fine_hbm, fine_list, fine_slot, fine_tr, theta_f, phi_f, mid_phase,
    mid_list, mid_slot, mid_tr, theta_m, phi_m, coarse_phase, coarse_list, coarse_tr,
    fine_in, mid_in, coarse_in,
    fpad, par, mrecv, crs, crecv, along1, lift1, along2, lift2,
    cosm, sinm, cosc, sinc, fine_mask, mid_mask, coarse_mask, fine_wide, mid_wide, coarse_wide,
    load_sem, fsend, frecv, msend, mrecv_sem, csend, crecv_sem,
):
    n = nb * nd
    b, d = lax.axis_index("box"), lax.axis_index("dir")
    me = b * nd + d
    held = fine_in.shape[0]
    t_mid, t_coarse = theta_f.shape[1], theta_m.shape[1]
    mid_tiles = par.shape[0]
    mlt = mid_tiles // nd
    ctiles = crecv.shape[1]
    ntile = t_coarse // ctiles
    share = n // ntile

    def device(i):
        return (lax.div(i, nd), lax.rem(i, nd))

    fine_load = pltpu.make_async_copy(fine_hbm, fpad.at[pl.ds(4, held)], load_sem)
    fine_load.start()
    barrier = pltpu.get_barrier_semaphore()

    def greet(j, _):
        pl.semaphore_signal(
            barrier, inc=1, device_id=device(lax.rem(me + 1 + j, n)), device_id_type=MESH
        )
        return 0

    lax.fori_loop(0, n - 1, greet, 0)

    bd1 = phi_blocks(phi_f[...], 2)
    k1 = kron_identity(theta_f[...], 16)
    bd2 = phi_blocks(phi_m[...], 1)
    k2 = kron_identity(theta_m[...], 8)
    angles = pack_rows(coarse_phase[...])
    cosc[...] = jnp.cos(angles)
    sinc[...] = jnp.sin(angles)
    angles = pack_rows(mid_phase[...])
    low8 = iota(angles.shape, 2) < LANES // 2
    for table, values in ((cosm, jnp.cos(angles)), (sinm, jnp.sin(angles))):
        turned = pltpu.roll(values, LANES // 2, 2)
        table[0] = jnp.where(low8, values, turned)
        table[1] = jnp.where(low8, turned, values)
    fine_slots = [fine_slot[d * held + c] for c in range(held)]
    row_presence(fine_mask, fine_list[...], me * held)
    row_presence(mid_mask, mid_list[...], b * mid_list.shape[0])
    column_presence(coarse_mask, coarse_list[...])
    repeat_rows(fine_wide, fine_tr)
    repeat_rows(mid_wide, mid_tr)
    repeat_rows(coarse_wide, coarse_tr)

    zeros4 = jnp.zeros((4,) + fpad.shape[1:], BF16)

    @pl.when(me == 0)
    def _():
        fpad[0:4] = zeros4

    @pl.when(me == n - 1)
    def _():
        fpad[4 + held:8 + held] = zeros4

    @pl.when(b == 0)
    def _():
        mrecv[0] = jnp.zeros(mrecv.shape[1:], BF16)

    @pl.when(b == nb - 1)
    def _():
        mrecv[nd + 1] = jnp.zeros(mrecv.shape[1:], BF16)

    crecv[0:4] = jnp.zeros((4,) + crecv.shape[1:], BF16)
    crecv[n + 4:n + 8] = jnp.zeros((4,) + crecv.shape[1:], BF16)

    fine_load.wait()

    for g in range(4):
        part = fpad[4:4 + held, :, g * LANES:(g + 1) * LANES]
        part = part.reshape(held // 8, 2, 4 * 32, LANES)
        pair = jnp.concatenate([part[:, 0], part[:, 1]], axis=-1).reshape(-1, 2 * LANES)
        out = dot(pair, bd1).astype(BF16)
        for i in range(4):
            along1[4 * g + i] = out[:, i * LANES:(i + 1) * LANES]
    for uk in range(8):
        rhs = jnp.concatenate(
            [
                along1[:, uk * 32:uk * 32 + 16, :].reshape(256, LANES),
                along1[:, uk * 32 + 16:uk * 32 + 32, :].reshape(256, LANES),
            ],
            axis=-1,
        )
        lift1[uk] = dot(k1, rhs).reshape(t_mid, 16, 2 * LANES)

    lower = iota((16, LANES), 1) < LANES // 2

    low1 = iota((1, LANES), 1) < LANES // 2
    half_mid = mid_tiles // 2

    def parents_step(v, _):
        place, step4 = lax.rem(v, half_mid), 4 * lax.div(v, half_mid)

        def phase_row(table, e, u, k):
            first = table[e, place, pl.ds(fine_slots[8 * u + k] + step4, 1), :]
            second = table[e, place, pl.ds(fine_slots[8 * u + 4 + k] + step4, 1), :]
            return jnp.where(low1, first, second)

        for u in range(2):
            sums = []
            for e in range(2):
                t2 = 2 * v + e
                real, imag = None, None
                for k in range(4):
                    uk = 4 * u + k
                    value = lift1[uk, t2]
                    vr, vi = value[:, :LANES], value[:, LANES:]
                    co = phase_row(cosm, e, u, k)
                    si = phase_row(sinm, e, u, k)
                    tr, ti = co * vr - si * vi, co * vi + si * vr
                    real = tr if real is None else real + tr
                    imag = ti if imag is None else imag + ti
                sums.append((real, imag))
            for c in range(2):
                s0, s1 = sums[0][c], sums[1][c]
                par[v, 2 * u, 16 * c:16 * c + 16, :] = jnp.where(
                    lower, s0, pltpu.roll(s1, LANES // 2, 1)
                ).astype(BF16)
                par[v, 2 * u + 1, 16 * c:16 * c + 16, :] = jnp.where(
                    lower, pltpu.roll(s0, LANES // 2, 1), s1
                ).astype(BF16)
        return 0

    lax.fori_loop(0, mid_tiles, parents_step, 0)

    pl.semaphore_wait(barrier, n - 1)

    def fine_copy(to_next):
        peer = me + 1 if to_next else me - 1
        return pltpu.make_async_remote_copy(
            src_ref=fpad.at[pl.ds(held, 4)] if to_next else fpad.at[pl.ds(4, 4)],
            dst_ref=fpad.at[pl.ds(0, 4)] if to_next else fpad.at[pl.ds(4 + held, 4)],
            send_sem=fsend.at[0 if to_next else 1],
            recv_sem=frecv.at[0 if to_next else 1],
            device_id=device(peer),
            device_id_type=MESH,
        )

    def mid_copy(dd, box, slot, sem):
        return pltpu.make_async_remote_copy(
            src_ref=par.at[pl.ds(dd * mlt, mlt)],
            dst_ref=mrecv.at[slot],
            send_sem=msend.at[sem],
            recv_sem=mrecv_sem.at[slot],
            device_id=(box, dd),
            device_id_type=MESH,
        )

    def coarse_copy(tile, dest):
        return pltpu.make_async_remote_copy(
            src_ref=crs.at[pl.ds(tile * ctiles, ctiles)],
            dst_ref=crecv.at[4 + me],
            send_sem=csend.at[dest],
            recv_sem=crecv_sem.at[me],
            device_id=device(dest),
            device_id_type=MESH,
        )

    def each_mid(act):
        def own(j, _):
            dd = lax.rem(d + 1 + j, nd)
            act(mid_copy(dd, b, 1 + d, dd))
            return 0

        lax.fori_loop(0, nd - 1, own, 0)

        @pl.when((d == nd - 1) & (b < nb - 1))
        def _():
            def up(dd, _):
                act(mid_copy(dd, b + 1, 0, nd + dd))
                return 0

            lax.fori_loop(0, nd, up, 0)

        @pl.when((d == 0) & (b > 0))
        def _():
            def down(dd, _):
                act(mid_copy(dd, b - 1, nd + 1, nd + dd))
                return 0

            lax.fori_loop(0, nd, down, 0)

    each_mid(lambda c: c.start())
    mrecv[1 + d] = par[pl.ds(d * mlt, mlt)]

    @pl.when(me < n - 1)
    def _():
        fine_copy(True).start()

    @pl.when(me > 0)
    def _():
        fine_copy(False).start()

    rows = par.shape[1] * par.shape[2]
    for g in range(mid_tiles // 2):
        lhs = jnp.concatenate(
            [par[2 * g].reshape(rows, LANES), par[2 * g + 1].reshape(rows, LANES)], axis=-1
        )
        out = dot(lhs, bd2)
        for i in range(4):
            along2[4 * g + i] = out[:, i * LANES:(i + 1) * LANES]
    for k in range(4):
        for cg in range(2):
            r0 = k * 32 + cg * 8
            rhs = jnp.concatenate(
                [
                    along2[:, r0:r0 + 8, :].reshape(256, LANES),
                    along2[:, r0 + 16:r0 + 24, :].reshape(256, LANES),
                ],
                axis=-1,
            ).astype(BF16)
            lift2[2 * k + cg] = dot(k2, rhs).reshape(t_coarse, 8, 2 * LANES)

    slots = [mid_slot[d * 4 + k] for k in range(4)]
    my_tile = lax.div(me, share)

    def coarse_step(j, _):
        tile = lax.rem(my_tile + ntile // 4 + j, ntile)
        for i in range(ctiles):
            t2 = tile * ctiles + i
            reals, imags = [None, None], [None, None]
            for k in range(4):
                row = pl.ds(slots[k] + 4 * lax.div(t2, t_coarse // 2), 1)
                co = cosc[lax.rem(t2, t_coarse // 2), row, :]
                si = sinc[lax.rem(t2, t_coarse // 2), row, :]
                for cg in range(2):
                    value = lift2[2 * k + cg, t2]
                    vr, vi = value[:, :LANES], value[:, LANES:]
                    tr, ti = co * vr - si * vi, co * vi + si * vr
                    reals[cg] = tr if k == 0 else reals[cg] + tr
                    imags[cg] = ti if k == 0 else imags[cg] + ti
            crs[t2, 0:16, :] = jnp.concatenate(reals, axis=0).astype(BF16)
            crs[t2, 16:32, :] = jnp.concatenate(imags, axis=0).astype(BF16)
        for r in range(share):
            dest = tile * share + r

            @pl.when(dest != me)
            def _():
                coarse_copy(tile, dest).start()

        return 0

    lax.fori_loop(0, ntile, coarse_step, 0)
    crecv[4 + me] = crs[pl.ds(my_tile * ctiles, ctiles)]

    @pl.when(me > 0)
    def _():
        fine_copy(True).wait_recv()

    @pl.when(me < n - 1)
    def _():
        fine_copy(False).wait_recv()

    def fine_store(i, lt, real, imag):
        fine_in[i, 0:16, lane_tile(lt)] = real
        fine_in[i, 16:32, lane_tile(lt)] = imag

    translate(
        held // 4,
        fine_in.shape[2] // LANES,
        lambda g, j, lt: fpad[4 * g + j, :, lane_tile(lt)],
        fine_mask,
        lambda s, c, lt: fine_wide[s, c, :, lane_tile(lt)],
        fine_store,
    )

    def mid_wait(slot):
        mid_copy(0, b, slot, 0).wait_recv()

    def own_wait(j, _):
        mid_wait(1 + lax.rem(d + 1 + j, nd))
        return 0

    lax.fori_loop(0, nd - 1, own_wait, 0)

    @pl.when(b > 0)
    def _():
        mid_wait(0)

    @pl.when(b < nb - 1)
    def _():
        mid_wait(nd + 1)

    def mid_store(i, lt, real, imag):
        mid_in[i, 0:16, lane_tile(lt)] = real
        mid_in[i, 16:32, lane_tile(lt)] = imag

    translate(
        nd,
        mlt,
        lambda g, j, lt: mrecv[g + j // 4, lt, j % 4],
        mid_mask,
        lambda s, c, lt: mid_wide[s, c, :, lane_tile(lt)],
        mid_store,
    )

    def coarse_wait(j, _):
        source = lax.rem(me + n - 1 - j, n)
        pltpu.make_async_remote_copy(
            src_ref=crs.at[pl.ds(0, ctiles)],
            dst_ref=crecv.at[4 + source],
            send_sem=csend.at[source],
            recv_sem=crecv_sem.at[source],
            device_id=device(source),
            device_id_type=MESH,
        ).wait_recv()
        return 0

    lax.fori_loop(0, n - 1, coarse_wait, 0)

    width = coarse_in.shape[2]
    if share == 1:

        def coarse_load(g, j, lt):
            return crecv[4 * g + j, lt]

        def coarse_store(i, lt, real, imag):
            coarse_in[i, 0:16, lane_tile(lt)] = real
            coarse_in[i, 16:32, lane_tile(lt)] = imag

        def coarse_factor(s, c, lt):
            return coarse_wide[s, c, :, lane_tile(lt)]

    else:
        turn = lax.rem(LANES - lax.rem(me, share) * width, LANES)

        def coarse_load(g, j, lt):
            return pltpu.roll(crecv[4 * g + j, lt].astype(F32), turn, 1)[:, :width]

        def coarse_store(i, lt, real, imag):
            coarse_in[i, 0:16, :] = real
            coarse_in[i, 16:32, :] = imag

        def coarse_factor(s, c, lt):
            return coarse_wide[s, c]

    translate(n // 4, ctiles, coarse_load, coarse_mask, coarse_factor, coarse_store)

    each_mid(lambda c: c.wait_send())

    @pl.when(me < n - 1)
    def _():
        fine_copy(True).wait_send()

    @pl.when(me > 0)
    def _():
        fine_copy(False).wait_send()

    def sent(j, _):
        dest = lax.rem(me + 1 + j, n)
        coarse_copy(lax.div(dest, share), dest).wait_send()
        return 0

    lax.fori_loop(0, n - 1, sent, 0)


def local(
    nb, nd,
    fine_out, fine_list, fine_slot, fine_translator, theta_up_fine, phi_up_fine, middle_phase,
    middle_list, middle_slot, middle_translator, theta_up_middle, phi_up_middle, coarse_phase,
    coarse_list, coarse_translator,
):
    n = nb * nd
    held, comps, fine_dirs = fine_out.shape
    t_mid, q_mid = theta_up_fine.shape[0], phi_up_fine.shape[0]
    t_coarse = theta_up_middle.shape[0]
    mid_phase = middle_phase.reshape(4, -1, LANES).transpose(1, 0, 2)
    co_phase = coarse_phase.reshape(4, -1, LANES).transpose(1, 0, 2)
    mid_tiles = t_mid * q_mid // LANES
    width = coarse_translator.shape[2]
    slots = fine_list.shape[1]
    ctiles = max(1, width // LANES)
    vmem = pl.BlockSpec(memory_space=pltpu.VMEM)
    smem = pl.BlockSpec(memory_space=pltpu.SMEM)
    dma = pltpu.SemaphoreType.DMA
    return pl.pallas_call(
        functools.partial(kernel, nb, nd),
        out_shape=(
            jax.ShapeDtypeStruct(fine_out.shape, BF16),
            jax.ShapeDtypeStruct((middle_list.shape[0], comps, middle_translator.shape[2]), BF16),
            jax.ShapeDtypeStruct((coarse_list.shape[0], comps, width), BF16),
        ),
        in_specs=[
            pl.BlockSpec(memory_space=pl.ANY), vmem, smem, vmem, vmem, vmem, vmem,
            vmem, smem, vmem, vmem, vmem, vmem, vmem, vmem,
        ],
        out_specs=(vmem, vmem, vmem),
        scratch_shapes=[
            pltpu.VMEM((held + 8, comps, fine_dirs), BF16),
            pltpu.VMEM((mid_tiles, 4, comps, LANES), BF16),
            pltpu.VMEM((nd + 2, mid_tiles // nd, 4, comps, LANES), BF16),
            pltpu.VMEM((t_coarse, comps, LANES), BF16),
            pltpu.VMEM((n + 8, ctiles, comps, LANES), BF16),
            pltpu.VMEM((theta_up_fine.shape[1], held // 2 * comps, LANES), BF16),
            pltpu.VMEM((held // 2, t_mid, 16, 2 * LANES), F32),
            pltpu.VMEM((theta_up_middle.shape[1], 4 * comps, LANES), F32),
            pltpu.VMEM((8, t_coarse, 8, 2 * LANES), F32),
            pltpu.VMEM((2, mid_tiles // 2, 8, LANES), F32),
            pltpu.VMEM((2, mid_tiles // 2, 8, LANES), F32),
            pltpu.VMEM((t_coarse // 2, 8, LANES), F32),
            pltpu.VMEM((t_coarse // 2, 8, LANES), F32),
            pltpu.VMEM((slots, held, 8, LANES), F32),
            pltpu.VMEM((slots, middle_list.shape[0], 8, LANES), F32),
            pltpu.VMEM((slots, coarse_list.shape[0], 8, LANES), F32),
            pltpu.VMEM((slots, 2, 8, fine_dirs), F32),
            pltpu.VMEM((slots, 2, 8, middle_translator.shape[2]), F32),
            pltpu.VMEM((slots, 2, 8, width), F32),
            dma, dma((2,)), dma((2,)), dma((2 * nd,)), dma((nd + 2,)), dma((n,)), dma((n,)),
        ],
        compiler_params=pltpu.CompilerParams(
            collective_id=0, has_side_effects=True, vmem_limit_bytes=48 * 1024 * 1024
        ),
        cost_estimate=pl.CostEstimate(
            flops=4_000_000_000, bytes_accessed=4_000_000, transcendentals=0
        ),
    )(
        fine_out, fine_list, fine_slot, fine_translator, theta_up_fine.T, phi_up_fine.T, mid_phase,
        middle_list, middle_slot, middle_translator, theta_up_middle.T, phi_up_middle.T, co_phase,
        coarse_list.T, coarse_translator,
    )


def solution(mesh):
    return jax.shard_map(
        functools.partial(local, mesh.shape["box"], mesh.shape["dir"]),
        mesh=mesh,
        in_specs=(
            P(("box", "dir"), None, None),
            P(("box", "dir"), None),
            P("box"),
            P(),
            P(),
            P(),
            P(),
            P("box", None),
            P("box"),
            P(None, None, "dir"),
            P(),
            P(),
            P(),
            P(),
            P(None, None, ("box", "dir")),
        ),
        out_specs=(
            P(("box", "dir"), None, None),
            P("box", None, "dir"),
            P(None, None, ("box", "dir")),
        ),
        check_vma=False,
    )
```

```python
import functools

import jax
import jax.numpy as jnp
from jax import lax
from jax.experimental import pallas as pl
from jax.experimental.pallas import tpu as pltpu
from jax.sharding import PartitionSpec as P

MAX_OFFSET = 7
LANES = 128
F32 = jnp.float32
BF16 = jnp.bfloat16
MESH = pl.DeviceIdType.MESH


def offsets_used():
    return list(range(-MAX_OFFSET, -1)) + list(range(2, MAX_OFFSET + 1))


def iota(shape, dim):
    return lax.broadcasted_iota(jnp.int32, shape, dim)


def one_hot(cond):
    return jnp.where(cond, 1.0, 0.0).astype(BF16)


def dot(a, b, dims=((1,), (0,))):
    return lax.dot_general(a, b, (dims, ((), ())), preferred_element_type=F32)


def kron_identity(matrix, width):
    cols, rows = matrix.shape
    shift = width.bit_length() - 1
    left = one_hot((iota((rows * width, rows), 0) >> shift) == iota((rows * width, rows), 1))
    right = one_hot(iota((cols, cols * width), 0) == (iota((cols, cols * width), 1) >> shift))
    full = dot(dot(left, matrix, ((1,), (1,))).astype(BF16), right)
    shape = (rows * width, cols * width)
    keep = (iota(shape, 0) & (width - 1)) == (iota(shape, 1) & (width - 1))
    return jnp.where(keep, full, 0.0).astype(BF16)


def phi_blocks(phi, pair):
    p, q = phi.shape
    thetas = 256 // (pair * p)
    rows, cols = pair * thetas * p, thetas * pair * q
    left = one_hot((iota((rows, p), 0) & (p - 1)) == iota((rows, p), 1))
    right = one_hot(iota((q, cols), 0) == (iota((q, cols), 1) & (q - 1)))
    full = dot(dot(left, phi).astype(BF16), right)
    shape = (rows, cols)
    r, c = iota(shape, 0), iota(shape, 1)
    ps, qs = p.bit_length() - 1, q.bit_length() - 1
    ths, prs = thetas.bit_length() - 1, pair.bit_length() - 1
    row_t, row_h = (r >> ps) & (thetas - 1), r >> (ps + ths)
    col_h, col_t = (c >> qs) & (pair - 1), c >> (qs + prs)
    return jnp.where((row_t == col_t) & (row_h == col_h), full, 0.0).astype(BF16)


def spread(mask, s, column):
    rows = column.shape[0]
    mask[s] = jnp.broadcast_to(column[:, :, None], (rows, 8, LANES))


def row_presence(mask, entries, first_box):
    ids = first_box + iota(entries.shape, 0)
    for s, offset in enumerate(offsets_used()):
        hit = jnp.where(entries == ids + offset, 1.0, 0.0)
        spread(mask, s, jnp.max(hit, axis=1, keepdims=True))


def column_presence(mask, entries):
    count = entries.shape[1]
    ids = iota(entries.shape, 1)
    eye = iota((count, count), 0) == iota((count, count), 1)
    for s, offset in enumerate(offsets_used()):
        hit = jnp.where(entries == ids + offset, 1.0, 0.0)
        row = jnp.max(hit, axis=0, keepdims=True)
        spread(mask, s, jnp.sum(jnp.where(eye, row, 0.0), axis=1, keepdims=True))


def repeat_rows(wide, factors):
    for s in range(factors.shape[0]):
        for c in range(2):
            wide[s, c] = jnp.broadcast_to(factors[s, c:c + 1, :], wide.shape[2:])


def pack_rows(table):
    half = table.shape[0] // 2
    return jnp.concatenate([table[:half], table[half:]], axis=1)


def translate(groups, tiles, load, mask_ref, factor, store):
    def step(it, _):
        g, lt = lax.div(it, tiles), lax.rem(it, tiles)
        sources = [load(g, j, lt).astype(F32) for j in range(12)]
        sources = [x.reshape(4, 8, x.shape[1]) for x in sources]
        width = sources[0].shape[2]
        for i in range(4):
            real, imag = None, None
            for s, offset in enumerate(offsets_used()):
                j = 4 + i + offset
                if j < 0 or j > 11:
                    continue
                m = mask_ref[s, 4 * g + i][:, :width]
                a, b = factor(s, 0, lt) * m, factor(s, 1, lt) * m
                pr, pi = sources[j][:2], sources[j][2:]
                tr, ti = a * pr - b * pi, a * pi + b * pr
                real = tr if real is None else real + tr
                imag = ti if imag is None else imag + ti
            real, imag = real.reshape(16, width), imag.reshape(16, width)
            store(4 * g + i, lt, real.astype(BF16), imag.astype(BF16))
        return 0

    lax.fori_loop(0, groups * tiles, step, 0)


def lane_tile(lt):
    return pl.ds(pl.multiple_of(lt * LANES, LANES), LANES)


def kernel(
    nb, nd, fine_hbm, *refs,
):
    smalls, refs = refs[:14], refs[14:]
    held_smalls, refs = refs[-15:-1], refs[:-15] + refs[-1:]
    climb(nb, nd, fine_hbm, smalls, held_smalls, *refs)


def climb(
    nb, nd, fine_hbm, smalls, held_smalls,
    fine_in, mid_in, coarse_in,
    fpad, par, mrecv, crs, crecv, along1, lift1, along2, lift2,
    cosm, sinm, cosc, sinc, fine_mask, mid_mask, coarse_mask, fine_wide, mid_wide, coarse_wide,
    load_sem, fsend, frecv, msend, mrecv_sem, csend, crecv_sem, small_sems,
):
    (
        fine_list, fine_slot, fine_tr, theta_f, phi_f, mid_phase,
        mid_list, mid_slot, mid_tr, theta_m, phi_m, coarse_phase, coarse_list, coarse_tr,
    ) = held_smalls
    n = nb * nd
    b, d = lax.axis_index("box"), lax.axis_index("dir")
    me = b * nd + d
    held = fine_in.shape[0]
    t_mid, t_coarse = theta_f.shape[1], theta_m.shape[1]
    mid_tiles = par.shape[0]
    mlt = mid_tiles // nd
    ctiles = crecv.shape[1]
    ntile = t_coarse // ctiles
    share = n // ntile

    def device(i):
        return (lax.div(i, nd), lax.rem(i, nd))

    fine_load = pltpu.make_async_copy(fine_hbm, fpad.at[pl.ds(4, held)], load_sem)
    fine_load.start()
    small_loads = [
        pltpu.make_async_copy(source, place, small_sems.at[i])
        for i, (source, place) in enumerate(zip(smalls, held_smalls))
    ]
    for load in small_loads:
        load.start()
    barrier = pltpu.get_barrier_semaphore()

    def greet(j, _):
        pl.semaphore_signal(
            barrier, inc=1, device_id=device(lax.rem(me + 1 + j, n)), device_id_type=MESH
        )
        return 0

    lax.fori_loop(0, n - 1, greet, 0)
    for load in small_loads:
        load.wait()

    bd1 = phi_blocks(phi_f[...], 2)
    k1 = kron_identity(theta_f[...], 16)
    bd2 = phi_blocks(phi_m[...], 1)
    k2 = kron_identity(theta_m[...], 8)
    angles = pack_rows(coarse_phase[...])
    cosc[...] = jnp.cos(angles)
    sinc[...] = jnp.sin(angles)
    angles = pack_rows(mid_phase[...])
    low8 = iota(angles.shape, 2) < LANES // 2
    for table, values in ((cosm, jnp.cos(angles)), (sinm, jnp.sin(angles))):
        turned = pltpu.roll(values, LANES // 2, 2)
        table[0] = jnp.where(low8, values, turned)
        table[1] = jnp.where(low8, turned, values)
    fine_slots = [fine_slot[d * held + c] for c in range(held)]
    row_presence(fine_mask, fine_list[...], me * held)
    row_presence(mid_mask, mid_list[...], b * mid_list.shape[0])
    column_presence(coarse_mask, coarse_list[...])
    repeat_rows(fine_wide, fine_tr)
    repeat_rows(mid_wide, mid_tr)
    repeat_rows(coarse_wide, coarse_tr)

    zeros4 = jnp.zeros((4,) + fpad.shape[1:], BF16)

    @pl.when(me == 0)
    def _():
        fpad[0:4] = zeros4

    @pl.when(me == n - 1)
    def _():
        fpad[4 + held:8 + held] = zeros4

    @pl.when(b == 0)
    def _():
        mrecv[0] = jnp.zeros(mrecv.shape[1:], BF16)

    @pl.when(b == nb - 1)
    def _():
        mrecv[nd + 1] = jnp.zeros(mrecv.shape[1:], BF16)

    crecv[0:4] = jnp.zeros((4,) + crecv.shape[1:], BF16)
    crecv[n + 4:n + 8] = jnp.zeros((4,) + crecv.shape[1:], BF16)

    fine_load.wait()

    for g in range(4):
        part = fpad[4:4 + held, :, g * LANES:(g + 1) * LANES]
        part = part.reshape(held // 8, 2, 4 * 32, LANES)
        pair = jnp.concatenate([part[:, 0], part[:, 1]], axis=-1).reshape(-1, 2 * LANES)
        out = dot(pair, bd1).astype(BF16)
        for i in range(4):
            along1[4 * g + i] = out[:, i * LANES:(i + 1) * LANES]
    for uk in range(8):
        rhs = jnp.concatenate(
            [
                along1[:, uk * 32:uk * 32 + 16, :].reshape(256, LANES),
                along1[:, uk * 32 + 16:uk * 32 + 32, :].reshape(256, LANES),
            ],
            axis=-1,
        )
        lift1[uk] = dot(k1, rhs).reshape(t_mid, 16, 2 * LANES)

    lower = iota((16, LANES), 1) < LANES // 2

    low1 = iota((1, LANES), 1) < LANES // 2
    half_mid = mid_tiles // 2

    def parents_step(v, _):
        place, step4 = lax.rem(v, half_mid), 4 * lax.div(v, half_mid)

        def phase_row(table, e, u, k):
            first = table[e, place, pl.ds(fine_slots[8 * u + k] + step4, 1), :]
            second = table[e, place, pl.ds(fine_slots[8 * u + 4 + k] + step4, 1), :]
            return jnp.where(low1, first, second)

        for u in range(2):
            sums = []
            for e in range(2):
                t2 = 2 * v + e
                real, imag = None, None
                for k in range(4):
                    uk = 4 * u + k
                    value = lift1[uk, t2]
                    vr, vi = value[:, :LANES], value[:, LANES:]
                    co = phase_row(cosm, e, u, k)
                    si = phase_row(sinm, e, u, k)
                    tr, ti = co * vr - si * vi, co * vi + si * vr
                    real = tr if real is None else real + tr
                    imag = ti if imag is None else imag + ti
                sums.append((real, imag))
            for c in range(2):
                s0, s1 = sums[0][c], sums[1][c]
                par[v, 2 * u, 16 * c:16 * c + 16, :] = jnp.where(
                    lower, s0, pltpu.roll(s1, LANES // 2, 1)
                ).astype(BF16)
                par[v, 2 * u + 1, 16 * c:16 * c + 16, :] = jnp.where(
                    lower, pltpu.roll(s0, LANES // 2, 1), s1
                ).astype(BF16)
        return 0

    lax.fori_loop(0, mid_tiles, parents_step, 0)

    pl.semaphore_wait(barrier, n - 1)

    def fine_copy(to_next):
        peer = me + 1 if to_next else me - 1
        return pltpu.make_async_remote_copy(
            src_ref=fpad.at[pl.ds(held, 4)] if to_next else fpad.at[pl.ds(4, 4)],
            dst_ref=fpad.at[pl.ds(0, 4)] if to_next else fpad.at[pl.ds(4 + held, 4)],
            send_sem=fsend.at[0 if to_next else 1],
            recv_sem=frecv.at[0 if to_next else 1],
            device_id=device(peer),
            device_id_type=MESH,
        )

    def mid_copy(dd, box, slot, sem):
        return pltpu.make_async_remote_copy(
            src_ref=par.at[pl.ds(dd * mlt, mlt)],
            dst_ref=mrecv.at[slot],
            send_sem=msend.at[sem],
            recv_sem=mrecv_sem.at[slot],
            device_id=(box, dd),
            device_id_type=MESH,
        )

    def coarse_copy(tile, dest):
        return pltpu.make_async_remote_copy(
            src_ref=crs.at[pl.ds(tile * ctiles, ctiles)],
            dst_ref=crecv.at[4 + me],
            send_sem=csend.at[dest],
            recv_sem=crecv_sem.at[me],
            device_id=device(dest),
            device_id_type=MESH,
        )

    def each_mid(act):
        def own(j, _):
            dd = lax.rem(d + 1 + j, nd)
            act(mid_copy(dd, b, 1 + d, dd))
            return 0

        lax.fori_loop(0, nd - 1, own, 0)

        @pl.when((d == nd - 1) & (b < nb - 1))
        def _():
            def up(dd, _):
                act(mid_copy(dd, b + 1, 0, nd + dd))
                return 0

            lax.fori_loop(0, nd, up, 0)

        @pl.when((d == 0) & (b > 0))
        def _():
            def down(dd, _):
                act(mid_copy(dd, b - 1, nd + 1, nd + dd))
                return 0

            lax.fori_loop(0, nd, down, 0)

    each_mid(lambda c: c.start())
    mrecv[1 + d] = par[pl.ds(d * mlt, mlt)]

    @pl.when(me < n - 1)
    def _():
        fine_copy(True).start()

    @pl.when(me > 0)
    def _():
        fine_copy(False).start()

    rows = par.shape[1] * par.shape[2]
    for g in range(mid_tiles // 2):
        lhs = jnp.concatenate(
            [par[2 * g].reshape(rows, LANES), par[2 * g + 1].reshape(rows, LANES)], axis=-1
        )
        out = dot(lhs, bd2)
        for i in range(4):
            along2[4 * g + i] = out[:, i * LANES:(i + 1) * LANES]
    for k in range(4):
        for cg in range(2):
            r0 = k * 32 + cg * 8
            rhs = jnp.concatenate(
                [
                    along2[:, r0:r0 + 8, :].reshape(256, LANES),
                    along2[:, r0 + 16:r0 + 24, :].reshape(256, LANES),
                ],
                axis=-1,
            ).astype(BF16)
            lift2[2 * k + cg] = dot(k2, rhs).reshape(t_coarse, 8, 2 * LANES)

    slots = [mid_slot[d * 4 + k] for k in range(4)]
    my_tile = lax.div(me, share)

    def coarse_step(j, _):
        tile = lax.rem(my_tile + ntile // 4 + j, ntile)
        for i in range(ctiles):
            t2 = tile * ctiles + i
            reals, imags = [None, None], [None, None]
            for k in range(4):
                row = pl.ds(slots[k] + 4 * lax.div(t2, t_coarse // 2), 1)
                co = cosc[lax.rem(t2, t_coarse // 2), row, :]
                si = sinc[lax.rem(t2, t_coarse // 2), row, :]
                for cg in range(2):
                    value = lift2[2 * k + cg, t2]
                    vr, vi = value[:, :LANES], value[:, LANES:]
                    tr, ti = co * vr - si * vi, co * vi + si * vr
                    reals[cg] = tr if k == 0 else reals[cg] + tr
                    imags[cg] = ti if k == 0 else imags[cg] + ti
            crs[t2, 0:16, :] = jnp.concatenate(reals, axis=0).astype(BF16)
            crs[t2, 16:32, :] = jnp.concatenate(imags, axis=0).astype(BF16)
        for r in range(share):
            dest = tile * share + r

            @pl.when(dest != me)
            def _():
                coarse_copy(tile, dest).start()

        return 0

    lax.fori_loop(0, ntile, coarse_step, 0)
    crecv[4 + me] = crs[pl.ds(my_tile * ctiles, ctiles)]

    @pl.when(me > 0)
    def _():
        fine_copy(True).wait_recv()

    @pl.when(me < n - 1)
    def _():
        fine_copy(False).wait_recv()

    def fine_store(i, lt, real, imag):
        fine_in[i, 0:16, lane_tile(lt)] = real
        fine_in[i, 16:32, lane_tile(lt)] = imag

    translate(
        held // 4,
        fine_in.shape[2] // LANES,
        lambda g, j, lt: fpad[4 * g + j, :, lane_tile(lt)],
        fine_mask,
        lambda s, c, lt: fine_wide[s, c, :, lane_tile(lt)],
        fine_store,
    )

    def mid_wait(slot):
        mid_copy(0, b, slot, 0).wait_recv()

    def own_wait(j, _):
        mid_wait(1 + lax.rem(d + 1 + j, nd))
        return 0

    lax.fori_loop(0, nd - 1, own_wait, 0)

    @pl.when(b > 0)
    def _():
        mid_wait(0)

    @pl.when(b < nb - 1)
    def _():
        mid_wait(nd + 1)

    def mid_store(i, lt, real, imag):
        mid_in[i, 0:16, lane_tile(lt)] = real
        mid_in[i, 16:32, lane_tile(lt)] = imag

    translate(
        nd,
        mlt,
        lambda g, j, lt: mrecv[g + j // 4, lt, j % 4],
        mid_mask,
        lambda s, c, lt: mid_wide[s, c, :, lane_tile(lt)],
        mid_store,
    )

    def coarse_wait(j, _):
        source = lax.rem(me + n - 1 - j, n)
        pltpu.make_async_remote_copy(
            src_ref=crs.at[pl.ds(0, ctiles)],
            dst_ref=crecv.at[4 + source],
            send_sem=csend.at[source],
            recv_sem=crecv_sem.at[source],
            device_id=device(source),
            device_id_type=MESH,
        ).wait_recv()
        return 0

    lax.fori_loop(0, n - 1, coarse_wait, 0)

    width = coarse_in.shape[2]
    if share == 1:

        def coarse_load(g, j, lt):
            return crecv[4 * g + j, lt]

        def coarse_store(i, lt, real, imag):
            coarse_in[i, 0:16, lane_tile(lt)] = real
            coarse_in[i, 16:32, lane_tile(lt)] = imag

        def coarse_factor(s, c, lt):
            return coarse_wide[s, c, :, lane_tile(lt)]

    else:
        turn = lax.rem(LANES - lax.rem(me, share) * width, LANES)

        def coarse_load(g, j, lt):
            return pltpu.roll(crecv[4 * g + j, lt].astype(F32), turn, 1)[:, :width]

        def coarse_store(i, lt, real, imag):
            coarse_in[i, 0:16, :] = real
            coarse_in[i, 16:32, :] = imag

        def coarse_factor(s, c, lt):
            return coarse_wide[s, c]

    translate(n // 4, ctiles, coarse_load, coarse_mask, coarse_factor, coarse_store)

    each_mid(lambda c: c.wait_send())

    @pl.when(me < n - 1)
    def _():
        fine_copy(True).wait_send()

    @pl.when(me > 0)
    def _():
        fine_copy(False).wait_send()

    def sent(j, _):
        dest = lax.rem(me + 1 + j, n)
        coarse_copy(lax.div(dest, share), dest).wait_send()
        return 0

    lax.fori_loop(0, n - 1, sent, 0)


def local(
    nb, nd,
    fine_out, fine_list, fine_slot, fine_translator, theta_up_fine, phi_up_fine, middle_phase,
    middle_list, middle_slot, middle_translator, theta_up_middle, phi_up_middle, coarse_phase,
    coarse_list, coarse_translator,
):
    n = nb * nd
    held, comps, fine_dirs = fine_out.shape
    t_mid, q_mid = theta_up_fine.shape[0], phi_up_fine.shape[0]
    t_coarse = theta_up_middle.shape[0]
    mid_phase = middle_phase.reshape(4, -1, LANES).transpose(1, 0, 2)
    co_phase = coarse_phase.reshape(4, -1, LANES).transpose(1, 0, 2)
    mid_tiles = t_mid * q_mid // LANES
    width = coarse_translator.shape[2]
    slots = fine_list.shape[1]
    ctiles = max(1, width // LANES)
    vmem = pl.BlockSpec(memory_space=pltpu.VMEM)
    hbm = pl.BlockSpec(memory_space=pltpu.HBM)
    smalls = (
        fine_list, fine_slot, fine_translator, theta_up_fine.T, phi_up_fine.T, mid_phase,
        middle_list, middle_slot, middle_translator, theta_up_middle.T, phi_up_middle.T, co_phase,
        coarse_list.T, coarse_translator,
    )
    dma = pltpu.SemaphoreType.DMA
    return pl.pallas_call(
        functools.partial(kernel, nb, nd),
        out_shape=(
            jax.ShapeDtypeStruct(fine_out.shape, BF16),
            jax.ShapeDtypeStruct((middle_list.shape[0], comps, middle_translator.shape[2]), BF16),
            jax.ShapeDtypeStruct((coarse_list.shape[0], comps, width), BF16),
        ),
        in_specs=[hbm] * (1 + len(smalls)),
        out_specs=(vmem, vmem, vmem),
        scratch_shapes=[
            pltpu.VMEM((held + 8, comps, fine_dirs), BF16),
            pltpu.VMEM((mid_tiles, 4, comps, LANES), BF16),
            pltpu.VMEM((nd + 2, mid_tiles // nd, 4, comps, LANES), BF16),
            pltpu.VMEM((t_coarse, comps, LANES), BF16),
            pltpu.VMEM((n + 8, ctiles, comps, LANES), BF16),
            pltpu.VMEM((theta_up_fine.shape[1], held // 2 * comps, LANES), BF16),
            pltpu.VMEM((held // 2, t_mid, 16, 2 * LANES), F32),
            pltpu.VMEM((theta_up_middle.shape[1], 4 * comps, LANES), F32),
            pltpu.VMEM((8, t_coarse, 8, 2 * LANES), F32),
            pltpu.VMEM((2, mid_tiles // 2, 8, LANES), F32),
            pltpu.VMEM((2, mid_tiles // 2, 8, LANES), F32),
            pltpu.VMEM((t_coarse // 2, 8, LANES), F32),
            pltpu.VMEM((t_coarse // 2, 8, LANES), F32),
            pltpu.VMEM((slots, held, 8, LANES), F32),
            pltpu.VMEM((slots, middle_list.shape[0], 8, LANES), F32),
            pltpu.VMEM((slots, coarse_list.shape[0], 8, LANES), F32),
            pltpu.VMEM((slots, 2, 8, fine_dirs), F32),
            pltpu.VMEM((slots, 2, 8, middle_translator.shape[2]), F32),
            pltpu.VMEM((slots, 2, 8, width), F32),
            dma, dma((2,)), dma((2,)), dma((2 * nd,)), dma((nd + 2,)), dma((n,)), dma((n,)),
            *[
                (pltpu.SMEM if x.ndim == 1 else pltpu.VMEM)(x.shape, x.dtype) for x in smalls
            ],
            dma((len(smalls),)),
        ],
        compiler_params=pltpu.CompilerParams(
            collective_id=0, has_side_effects=True, vmem_limit_bytes=64 * 1024 * 1024
        ),
        cost_estimate=pl.CostEstimate(
            flops=4_000_000_000, bytes_accessed=4_000_000, transcendentals=0
        ),
    )(fine_out, *smalls)


def solution(mesh):
    return jax.shard_map(
        functools.partial(local, mesh.shape["box"], mesh.shape["dir"]),
        mesh=mesh,
        in_specs=(
            P(("box", "dir"), None, None),
            P(("box", "dir"), None),
            P("box"),
            P(),
            P(),
            P(),
            P(),
            P("box", None),
            P("box"),
            P(None, None, "dir"),
            P(),
            P(),
            P(),
            P(),
            P(None, None, ("box", "dir")),
        ),
        out_specs=(
            P(("box", "dir"), None, None),
            P("box", None, "dir"),
            P(None, None, ("box", "dir")),
        ),
        check_vma=False,
    )
```
